32 devices in a mesh: groups: 2 (over y), dp: 4 (over x, core), tensor: 4 (over z).
Axes of the slice: x: 2, y: 2, z: 4, core: 2. Of those that a mesh axis runs over, the one named last changes fastest.
Arguments:
- tokens: bfloat16 [64, 8192], P(('groups', 'tensor'), 'dp'), parts along dimension 0, may hold values from -6 to 6
- basis: bfloat16 [8192, 1024], P('dp'), may hold values from -0.0625 to 0.0625
- gate_weight: bfloat16 [8192, 16384], P('dp', 'tensor'), may hold values from -0.0625 to 0.0625
- up_weight: bfloat16 [8192, 16384], P('dp', 'tensor'), may hold values from -0.0625 to 0.0625
- down_weight: bfloat16 [16384, 8192], P('tensor', 'dp'), may hold values from -0.046875 to 0.046875
Outputs:
- mixed: bfloat16 [64, 8192], P(('groups', 'tensor'), 'dp'), parts along dimension 0
The draws below stay inside these ranges and needn't reach their ends.
There are 2 independent parts, one for each index of `groups`. The reference program is written for one: setup_inputs(seed, part) draws one part's arguments, and reference() takes and returns one part's arrays. A program takes and returns all parts, laid end to end along the dimension named above; an argument that names none is the same for every part. Nothing has to cross between parts.
All inputs are finite; a program needn't handle non-finite values.
Results may differ from the reference program's by a relative error of at most 0.0095.
Values may be sent and summed in bfloat16 or wider, within the bound.
No kernel may reach another device: no remote copies, remote signals or barrier semaphores. Data moves between devices by JAX's collectives and lax.ppermute only.
A program may use at most 128 MiB of HBM per device.

```python
import jax
import jax.numpy as jnp
from jax import lax

D = 8192
FF = 16384
R = 1024
TOKENS = 32


def block_levels(rng, extent, cuts, least, largest):
    def one(axis_at, parts):
        draws = jax.random.uniform(jax.random.fold_in(jax.random.fold_in(rng, 6), axis_at), (parts,), jnp.float32, least / len(cuts), largest / len(cuts))
        return jnp.repeat(jnp.exp(draws), extent[axis_at] // parts).reshape((-1,) + (1,) * (len(extent) - axis_at - 1))

    factor_of = one(*cuts[0])
    for cut in cuts[1:]:
        factor_of = factor_of * one(*cut)
    return factor_of


def gaussian(key, extent, deviation, most, pieces=(), kind=jnp.bfloat16):
    level = block_levels(key, extent, pieces, -0.22, 0.18) if pieces else 1.0
    result = jax.random.normal(key, extent, jnp.float32) * deviation * level
    return jnp.minimum(jnp.maximum(result, -most), most).astype(kind)


def setup_inputs(seed: int = 0, part: int = 0) -> dict:
    keys = jax.random.split(jax.random.key(seed), 6)
    part_keys = jax.random.split(jax.random.fold_in(keys[5], part), 6)
    return {
        "tokens": gaussian(part_keys[0], (TOKENS, D), 1.0, 6.0, ((0, 4), (1, 4))),
        "basis": gaussian(keys[1], (D, R), D ** -0.5, 0.0625, ((0, 4),)),
        "gate_weight": gaussian(keys[2], (D, FF), D ** -0.5, 0.0625, ((0, 4), (1, 4))),
        "up_weight": gaussian(keys[3], (D, FF), D ** -0.5, 0.0625, ((0, 4), (1, 4))),
        "down_weight": gaussian(keys[4], (FF, D), FF ** -0.5, 0.046875, ((0, 4), (1, 4))),
    }


def reference(tokens, basis, gate_weight, up_weight, down_weight):
    factor = (D / R) ** 0.5
    code_rows = jnp.dot(tokens, basis, preferred_element_type=jnp.float32).astype(jnp.bfloat16)
    restored = (factor * jnp.dot(code_rows, basis.T, preferred_element_type=jnp.float32)).astype(jnp.bfloat16)
    gate = jnp.dot(restored, gate_weight, preferred_element_type=jnp.float32)
    up_sum = jnp.dot(restored, up_weight, preferred_element_type=jnp.float32)
    hidden = (jax.nn.silu(gate) * up_sum).astype(jnp.bfloat16)
    projected = jnp.dot(hidden, down_weight, preferred_element_type=jnp.float32)
    out_codes = jnp.dot(projected, basis.astype(jnp.float32), precision=lax.Precision.HIGHEST).astype(jnp.bfloat16)
    return (factor * jnp.dot(out_codes, basis.T, preferred_element_type=jnp.float32)).astype(jnp.bfloat16)
```

```python
import functools

import jax
import jax.numpy as jnp
from jax import lax
from jax.experimental import pallas as pl
from jax.experimental.pallas import tpu as pltpu
from jax.sharding import PartitionSpec as P

D = 8192
R = 1024
F32 = jnp.float32
BF16 = jnp.bfloat16
LIMIT = 6 * 1024 * 1024
VMEM = pl.BlockSpec(memory_space=pltpu.VMEM)
SMEM = pl.BlockSpec(memory_space=pltpu.SMEM)


def call(body, out, microseconds, scalars, *arrays, scratch=(), hold=0):
    inputs = len(scalars) + len(arrays)
    kept = arrays[len(arrays) - hold :] if hold else ()

    def run(*refs):
        body(*refs[: inputs + 1], *refs[inputs + 1 + hold :])

    got = pl.pallas_call(
        run,
        out_shape=[out] + [jax.ShapeDtypeStruct(a.shape, a.dtype) for a in kept],
        in_specs=[SMEM] * len(scalars) + [VMEM] * len(arrays),
        out_specs=[VMEM] * (1 + hold),
        scratch_shapes=list(scratch),
        input_output_aliases={inputs - hold + i: 1 + i for i in range(hold)},
        cost_estimate=pl.CostEstimate(flops=0, bytes_accessed=int(microseconds * 3.69e6), transcendentals=0),
        compiler_params=pltpu.CompilerParams(vmem_limit_bytes=LIMIT),
    )(*scalars, *[pin(a) if a.size > 2**20 else a for a in arrays])
    return got if hold else got[0]


def pin(array):
    return pltpu.with_memory_space_constraint(array, pltpu.VMEM)


def swap(value, axis, mask, size):
    return lax.ppermute(value, axis, [(i, i ^ mask) for i in range(size)])


def tile_of(extent, most):
    tile = most
    while extent % tile:
        tile //= 2
    return tile


def dot(a, b):
    return jnp.dot(a, b, preferred_element_type=F32)


def dot_t(a, b):
    return lax.dot_general(a, b, (((1,), (1,)), ((), ())), preferred_element_type=F32)


def add_body(a_ref, b_ref, out_ref):
    out_ref[...] = (a_ref[...].astype(F32) + b_ref[...].astype(F32)).astype(BF16)


def join_body(a_ref, b_ref, out_ref):
    rows = a_ref.shape[0]
    out_ref[:rows] = a_ref[...]
    out_ref[rows:] = b_ref[...]


def code_body(x_ref, basis_ref, out_ref):
    tile = tile_of(R, 512)
    for t in range(0, R, tile):
        out_ref[:, t : t + tile] = dot(x_ref[...], basis_ref[:, t : t + tile]).astype(BF16)


def decode_body(codes_ref, basis_ref, out_ref, *, factor):
    width = basis_ref.shape[0]
    tile = tile_of(width, 512)
    for t in range(0, width, tile):
        out_ref[:, t : t + tile] = (factor * dot_t(codes_ref[...], basis_ref[t : t + tile, :])).astype(BF16)


def wide_body(x_ref, weight_ref, out_ref):
    tile = tile_of(out_ref.shape[1], 512)
    for t in range(0, out_ref.shape[1], tile):
        out_ref[:, t : t + tile] = dot(x_ref[...], weight_ref[:, t : t + tile]).astype(BF16)


def down_first_body(start_ref, h_ref, down_ref, out_ref):
    depth, width = h_ref.shape[1], out_ref.shape[1]
    tile = tile_of(width, 512)
    at = pl.ds(pl.multiple_of(start_ref[0], 128), depth)
    for t in range(0, width, tile):
        out_ref[:, t : t + tile] = dot(h_ref[...], down_ref[at, t : t + tile])


def down_last_body(start_ref, h_ref, down_ref, acc_ref, basis_ref, out_ref, rows_ref):
    depth, width = h_ref.shape[1], acc_ref.shape[1]
    tile = tile_of(width, 512)
    at = pl.ds(pl.multiple_of(start_ref[0], 128), depth)
    for t in range(0, width, tile):
        rows_ref[:, t : t + tile] = (
            acc_ref[:, t : t + tile] + dot(h_ref[...], down_ref[at, t : t + tile])
        ).astype(BF16)
    tile = tile_of(R, 512)
    for t in range(0, R, tile):
        out_ref[:, t : t + tile] = dot(rows_ref[...], basis_ref[:, t : t + tile]).astype(BF16)


def shards(tokens, basis, gate_weight, up_weight, down_weight, *, dp, tensor):
    factor = (D / R) ** 0.5
    local = tokens.shape[0]
    rows = local * tensor
    width = tokens.shape[1]
    ff = gate_weight.shape[1]
    core = lax.axis_index("dp") % 2
    sds = jax.ShapeDtypeStruct

    codes = call(code_body, sds((local, R), BF16), 1, (), tokens, basis)
    mask = 1
    while mask < dp:
        other = swap(codes, "dp", mask, dp)
        codes = call(add_body, sds(codes.shape, BF16), 1.3 if mask == 1 else 3.8, (), codes, other)
        mask *= 2
    mask = 1
    while mask < tensor:
        other = swap(codes, "tensor", mask, tensor)
        codes = call(join_body, sds((2 * codes.shape[0], R), BF16), 4.5, (), codes, other)
        mask *= 2
    restored = call(functools.partial(decode_body, factor=factor), sds((rows, width), BF16), 1, (), codes, basis)

    half = ff // 2
    mine = (core * half).astype(jnp.int32)
    theirs = ((1 - core) * half).astype(jnp.int32)
    sums = []
    for weight in (gate_weight, up_weight):
        part = call(wide_body, sds((rows, ff), BF16), 4, (), restored, weight)
        kept = lax.dynamic_slice_in_dim(part, mine, half, 1)
        got = swap(lax.dynamic_slice_in_dim(part, theirs, half, 1), "dp", 1, dp)
        sums.append((kept.astype(F32) + got.astype(F32)).astype(BF16))
    mask = 2
    while mask < dp:
        sums = [(s.astype(F32) + swap(s, "dp", mask, dp).astype(F32)).astype(F32 if 2 * mask == dp else BF16) for s in sums]
        mask *= 2
    gate, up = sums
    own = (gate.astype(F32) / (1 + jnp.exp(-gate.astype(F32))) * up.astype(F32)).astype(BF16)
    away = swap(own, "dp", 1, dp)
    acc = call(down_first_body, sds((rows, width), F32), 2, (mine.reshape(1),), own, down_weight)
    codes = call(
        down_last_body,
        sds((rows, R), BF16),
        3,
        (theirs.reshape(1),),
        away,
        down_weight,
        acc,
        basis,
        scratch=[pltpu.VMEM((rows, width), BF16)],
    )
    mask = tensor // 2
    while mask:
        top = codes.shape[0] // 2
        other = swap(codes[top:], "tensor", mask, tensor)
        codes = (codes[:top].astype(F32) + other.astype(F32)).astype(BF16)
        mask //= 2
    mask = dp // 2
    while mask:
        other = swap(codes, "dp", mask, dp)
        codes = (codes.astype(F32) + other.astype(F32)).astype(BF16)
        mask //= 2
    return call(
        functools.partial(decode_body, factor=factor), sds((local, width), BF16), 1, (), codes, basis
    )


def solution(mesh):
    placed = (
        P(("groups", "tensor"), "dp"),
        P("dp", None),
        P("dp", "tensor"),
        P("dp", "tensor"),
        P("tensor", "dp"),
    )
    return jax.shard_map(
        functools.partial(shards, dp=mesh.shape["dp"], tensor=mesh.shape["tensor"]),
        mesh=mesh,
        in_specs=placed,
        out_specs=P(("groups", "tensor"), "dp"),
        check_vma=False,
    )
```

```python
import functools

import jax
import jax.numpy as jnp
from jax import lax
from jax.experimental import pallas as pl
from jax.experimental.pallas import tpu as pltpu
from jax.sharding import PartitionSpec as P

D = 8192
R = 1024
F32 = jnp.float32
BF16 = jnp.bfloat16
LIMIT = 2 * 1024 * 1024
PIECES = 4
WAIT = 30
SUM = 6
PAIR = 1
VMEM = pl.BlockSpec(memory_space=pltpu.VMEM)
HBM = pl.BlockSpec(memory_space=pltpu.HBM)
sds = jax.ShapeDtypeStruct


def call(body, out, microseconds, *arrays, scratch=(), fixed=()):
    many = isinstance(out, list)
    return pl.pallas_call(
        body,
        out_shape=out,
        in_specs=[HBM if i in fixed else VMEM for i in range(len(arrays))],
        out_specs=[VMEM] * len(out) if many else VMEM,
        scratch_shapes=list(scratch),
        cost_estimate=pl.CostEstimate(flops=int(microseconds * 1.15e9), bytes_accessed=2**16, transcendentals=0),
        compiler_params=pltpu.CompilerParams(vmem_limit_bytes=LIMIT),
    )(*[pltpu.with_memory_space_constraint(a, pltpu.HBM) if i in fixed else a for i, a in enumerate(arrays)])


def swap(value, axis, mask, size):
    return lax.ppermute(value, axis, [(i, i ^ mask) for i in range(size)])


def tile_of(extent, most):
    tile = most
    while extent % tile:
        tile //= 2
    return tile


def dot(a, b):
    return jnp.dot(a, b, preferred_element_type=F32)


def dot_t(a, b):
    return lax.dot_general(a, b, (((1,), (1,)), ((), ())), preferred_element_type=F32)


def core_index():
    return lax.rem(lax.axis_index("dp"), 2)


def code_body(x_ref, basis_ref, out_ref, held_ref, tokens_ref, sems):
    deep = basis_ref.shape[0] // PIECES
    first = pltpu.make_async_copy(x_ref, tokens_ref, sems.at[PIECES])
    first.start()
    copies = []
    for p in range(PIECES):
        at = pl.ds(p * deep, deep)
        copies.append(pltpu.make_async_copy(basis_ref.at[at], held_ref.at[at], sems.at[p]))
        copies[-1].start()
    first.wait()
    for p in range(PIECES):
        copies[p].wait()
        part = dot(tokens_ref[:, p * deep : (p + 1) * deep], held_ref[p * deep : (p + 1) * deep, :])
        out_ref[...] = part if p == 0 else out_ref[...] + part


def add_body(a_ref, b_ref, *out_refs):
    total = a_ref[...] + b_ref[...].astype(F32)
    for out_ref in out_refs:
        out_ref[...] = total.astype(out_ref.dtype)


def half_body(a_ref, b_ref, keep_ref, send_ref):
    top = keep_ref.shape[0]
    keep_ref[...] = a_ref[:top] + b_ref[:top].astype(F32)
    send_ref[...] = (a_ref[top:] + b_ref[top:].astype(F32)).astype(BF16)


def join_body(a_ref, b_ref, out_ref):
    rows = a_ref.shape[0]
    out_ref[:rows] = a_ref[...]
    out_ref[rows:] = b_ref[...]


def hidden_body(a_ref, b_ref, out_ref):
    half = out_ref.shape[1]
    gate = a_ref[:, :half] + b_ref[:, :half].astype(F32)
    up = a_ref[:, half:] + b_ref[:, half:].astype(F32)
    out_ref[...] = (gate / (1 + jnp.exp(-gate)) * up).astype(BF16)


def decode(codes, basis_ref, out_ref):
    factor = (D / R) ** 0.5
    width = basis_ref.shape[0]
    tile = tile_of(width, 512)
    for t in range(0, width, tile):
        out_ref[:, t : t + tile] = (factor * dot_t(codes, basis_ref[t : t + tile, :])).astype(BF16)


def restore_body(codes_ref, basis_ref, out_ref):
    decode(codes_ref[...], basis_ref, out_ref)


def final_body(a_ref, b_ref, basis_ref, out_ref):
    decode((a_ref[...] + b_ref[...]).astype(BF16), basis_ref, out_ref)


def pair_body(x_ref, gate_ref, up_ref, *refs, start):
    keep_ref, send_ref = refs[-2:]
    half = keep_ref.shape[1] // 2
    tile = tile_of(half, 512)
    core = core_index()
    for out_ref, which in ((send_ref, 1 - core), (keep_ref, core)):
        for t in range(0, half, tile):
            at = pl.ds(pl.multiple_of(start + t + which * half, 128), tile)
            out_ref[:, t : t + tile] = dot(x_ref[...], gate_ref[:, at]).astype(out_ref.dtype)
            out_ref[:, half + t : half + t + tile] = dot(x_ref[...], up_ref[:, at]).astype(out_ref.dtype)


def down_body(*refs, start, half, own, away, first):
    h_refs, (weight_ref, *acc, out_ref) = refs[: own + away], refs[own + away :]
    core = core_index()
    which = ([core] if own else []) + ([1 - core] if away else [])
    width = out_ref.shape[1]
    tile = tile_of(width, 512)
    for t in range(0, width, tile):
        total = None if first else acc[0][:, t : t + tile]
        for h_ref, w in zip(h_refs, which):
            at = pl.ds(pl.multiple_of(start + w * half, 16), half)
            part = dot(h_ref[...], weight_ref[at, t : t + tile])
            total = part if total is None else total + part
        out_ref[:, t : t + tile] = total.astype(out_ref.dtype)


def last_body(h_ref, weight_ref, acc_ref, basis_ref, keep_ref, send_ref, rows_ref, *, start, half):
    down_body(h_ref, weight_ref, acc_ref, rows_ref, start=start, half=half, own=0, away=1, first=False)
    top = keep_ref.shape[0]
    tile = tile_of(R, 512)
    for t in range(0, R, tile):
        part = dot(rows_ref[...], basis_ref[:, t : t + tile])
        keep_ref[:, t : t + tile] = part[:top]
        send_ref[:, t : t + tile] = part[top:].astype(BF16)


def both(shape):
    return [sds(shape, F32), sds(shape, BF16)]


def shards(tokens, basis, gate_weight, up_weight, down_weight, *, dp, tensor):
    local, width = tokens.shape
    rows = local * tensor
    ff = gate_weight.shape[1]

    codes, basis = call(
        code_body,
        [sds((local, R), F32), sds(basis.shape, BF16)],
        1,
        tokens,
        basis,
        scratch=[pltpu.VMEM(tokens.shape, BF16), pltpu.SemaphoreType.DMA((PIECES + 1,))],
        fixed=(0, 1),
    )
    codes, send = call(add_body, both(codes.shape), WAIT, codes, swap(codes, "dp", 1, dp))
    mask = 2
    while 2 * mask < dp:
        codes, send = call(add_body, both(codes.shape), 0.1, codes, swap(send, "dp", mask, dp))
        mask *= 2
    codes = call(add_body, sds(codes.shape, BF16), 0.1, codes, swap(send, "dp", mask, dp))
    mask = 1
    while mask < tensor:
        codes = call(
            join_body, sds((2 * codes.shape[0], R), BF16), 0.1, codes, swap(codes, "tensor", mask, tensor)
        )
        mask *= 2
    restored = call(restore_body, sds((rows, width), BF16), 0.5, codes, basis)

    shares = SHARES if ff % 1024 == 0 else (1, 1)
    spans, at = [], 0
    for share in shares:
        spans.append((at, ff * share // sum(shares)))
        at += spans[-1][1]
    sums = []
    after = []
    for q, (start, span) in enumerate(spans):
        keep, send = call(
            functools.partial(pair_body, start=start),
            both((rows, span)),
            PAIR * span / ff,
            restored,
            gate_weight,
            up_weight,
            *after,
        )
        sums.append((keep, swap(send, "dp", 1, dp)))
        after = [keep]
        if q > 0:
            sums[q - 1] = call(add_body, both((rows, spans[q - 1][1])), SUM, *sums[q - 1])
            after.append(sums[q - 1][1])
    sums[-1] = call(add_body, both((rows, spans[-1][1])), SUM, *sums[-1])
    acc = None
    for (start, span), (total, send) in zip(spans, sums):
        mask = 2
        while 2 * mask < dp:
            total, send = call(add_body, both(total.shape), 0.1, total, swap(send, "dp", mask, dp))
            mask *= 2
        half = span // 2
        own = call(hidden_body, sds((rows, half), BF16), 0.1, total, swap(send, "dp", mask, dp))
        away = swap(own, "dp", 1, dp)
        time = 3 * span / ff
        shape = sds((rows, width), F32)
        if start + span < ff:
            body = functools.partial(down_body, start=start, half=half, own=1, away=1, first=acc is None)
            acc = call(body, shape, time, own, away, down_weight, *([] if acc is None else [acc]))
        else:
            body = functools.partial(down_body, start=start, half=half, own=1, away=0, first=False)
            acc = call(body, shape, time / 2, own, down_weight, acc)
            codes, send = call(
                functools.partial(last_body, start=start, half=half),
                [sds((rows // 2, R), F32), sds((rows // 2, R), BF16)],
                1,
                away,
                down_weight,
                acc,
                basis,
                scratch=[pltpu.VMEM((rows, width), BF16)],
            )

    mask = tensor // 2
    while mask > 1:
        top = codes.shape[0] // 2
        codes, send = call(
            half_body, [sds((top, R), F32), sds((top, R), BF16)], 0.1, codes, swap(send, "tensor", mask, tensor)
        )
        mask //= 2
    codes, send = call(add_body, both(codes.shape), 0.1, codes, swap(send, "tensor", 1, tensor))
    mask = dp // 2
    while mask > 1:
        codes, send = call(add_body, both(codes.shape), 0.1, codes, swap(send, "dp", mask, dp))
        mask //= 2
    return call(final_body, sds((local, width), BF16), 1, codes, swap(codes, "dp", 1, dp), basis)


SHARES = (2, 1, 1)


def solution(mesh):
    placed = (
        P(("groups", "tensor"), "dp"),
        P("dp", None),
        P("dp", "tensor"),
        P("dp", "tensor"),
        P("tensor", "dp"),
    )
    return jax.shard_map(
        functools.partial(shards, dp=mesh.shape["dp"], tensor=mesh.shape["tensor"]),
        mesh=mesh,
        in_specs=placed,
        out_specs=P(("groups", "tensor"), "dp"),
        check_vma=False,
    )
```

```python
import functools

import jax
import jax.numpy as jnp
from jax import lax
from jax.experimental import pallas as pl
from jax.experimental.pallas import tpu as pltpu
from jax.sharding import PartitionSpec as P

D = 8192
R = 1024
F32 = jnp.float32
BF16 = jnp.bfloat16
LIMIT = 2 * 1024 * 1024
PIECES = 4
WAIT = 30
SUMS = (0.3, 0.3, 0.3)
PAIR = 6
HIDDEN = (5, 0.1, 0.1)
DOWN = 3
VMEM = pl.BlockSpec(memory_space=pltpu.VMEM)
HBM = pl.BlockSpec(memory_space=pltpu.HBM)
sds = jax.ShapeDtypeStruct


def call(body, out, microseconds, *arrays, scratch=(), fixed=()):
    many = isinstance(out, list)
    return pl.pallas_call(
        body,
        out_shape=out,
        in_specs=[HBM if i in fixed else VMEM for i in range(len(arrays))],
        out_specs=[VMEM] * len(out) if many else VMEM,
        scratch_shapes=list(scratch),
        cost_estimate=pl.CostEstimate(flops=int(microseconds * 1.15e9), bytes_accessed=2**16, transcendentals=0),
        compiler_params=pltpu.CompilerParams(vmem_limit_bytes=LIMIT),
    )(*[pltpu.with_memory_space_constraint(a, pltpu.HBM) if i in fixed else a for i, a in enumerate(arrays)])


def swap(value, axis, mask, size):
    return lax.ppermute(value, axis, [(i, i ^ mask) for i in range(size)])


def tile_of(extent, most):
    tile = most
    while extent % tile:
        tile //= 2
    return tile


def dot(a, b):
    return jnp.dot(a, b, preferred_element_type=F32)


def dot_t(a, b):
    return lax.dot_general(a, b, (((1,), (1,)), ((), ())), preferred_element_type=F32)


def core_index():
    return lax.rem(lax.axis_index("dp"), 2)


def code_body(x_ref, basis_ref, out_ref, held_ref, tokens_ref, sems):
    deep = basis_ref.shape[0] // PIECES
    first = pltpu.make_async_copy(x_ref, tokens_ref, sems.at[PIECES])
    first.start()
    copies = []
    for p in range(PIECES):
        at = pl.ds(p * deep, deep)
        copies.append(pltpu.make_async_copy(basis_ref.at[at], held_ref.at[at], sems.at[p]))
        copies[-1].start()
    first.wait()
    for p in range(PIECES):
        copies[p].wait()
        part = dot(tokens_ref[:, p * deep : (p + 1) * deep], held_ref[p * deep : (p + 1) * deep, :])
        out_ref[...] = part if p == 0 else out_ref[...] + part


def add_body(a_ref, b_ref, *refs, outs=1):
    total = a_ref[...] + b_ref[...].astype(F32)
    for out_ref in refs[-outs:]:
        out_ref[...] = total.astype(out_ref.dtype)


add_two_body = functools.partial(add_body, outs=2)


def half_body(a_ref, b_ref, keep_ref, send_ref):
    top = keep_ref.shape[0]
    keep_ref[...] = a_ref[:top] + b_ref[:top].astype(F32)
    send_ref[...] = (a_ref[top:] + b_ref[top:].astype(F32)).astype(BF16)


def join_body(a_ref, b_ref, out_ref):
    rows = a_ref.shape[0]
    out_ref[:rows] = a_ref[...]
    out_ref[rows:] = b_ref[...]


def hidden_body(a_ref, b_ref, *refs):
    out_ref = refs[-1]
    half = out_ref.shape[1]
    gate = a_ref[:, :half] + b_ref[:, :half].astype(F32)
    up = a_ref[:, half:] + b_ref[:, half:].astype(F32)
    out_ref[...] = (gate / (1 + jnp.exp(-gate)) * up).astype(BF16)


def decode(codes, basis_ref, out_ref):
    factor = (D / R) ** 0.5
    width = basis_ref.shape[0]
    tile = tile_of(width, 512)
    for t in range(0, width, tile):
        out_ref[:, t : t + tile] = (factor * dot_t(codes, basis_ref[t : t + tile, :])).astype(BF16)


def restore_body(codes_ref, basis_ref, out_ref):
    decode(codes_ref[...], basis_ref, out_ref)


def final_body(a_ref, b_ref, basis_ref, out_ref):
    decode((a_ref[...] + b_ref[...]).astype(BF16), basis_ref, out_ref)


def pair_body(x_ref, gate_ref, up_ref, *refs, start):
    keep_ref, send_ref = refs[-2:]
    half = keep_ref.shape[1] // 2
    tile = tile_of(half, 512)
    core = core_index()
    for out_ref, which in ((send_ref, 1 - core), (keep_ref, core)):
        for t in range(0, half, tile):
            at = pl.ds(pl.multiple_of(start + t + which * half, 128), tile)
            out_ref[:, t : t + tile] = dot(x_ref[...], gate_ref[:, at]).astype(out_ref.dtype)
            out_ref[:, half + t : half + t + tile] = dot(x_ref[...], up_ref[:, at]).astype(out_ref.dtype)


def down_body(*refs, start, half, own, away, first):
    h_refs, (weight_ref, *acc, out_ref) = refs[: own + away], refs[own + away :]
    core = core_index()
    which = ([core] if own else []) + ([1 - core] if away else [])
    width = out_ref.shape[1]
    tile = tile_of(width, 512)
    for t in range(0, width, tile):
        total = None if first else acc[0][:, t : t + tile]
        for h_ref, w in zip(h_refs, which):
            at = pl.ds(pl.multiple_of(start + w * half, 16), half)
            part = dot(h_ref[...], weight_ref[at, t : t + tile])
            total = part if total is None else total + part
        out_ref[:, t : t + tile] = total.astype(out_ref.dtype)


def last_body(h_ref, weight_ref, acc_ref, basis_ref, keep_ref, send_ref, rows_ref, *, start, half):
    down_body(h_ref, weight_ref, acc_ref, rows_ref, start=start, half=half, own=0, away=1, first=False)
    top = keep_ref.shape[0]
    tile = tile_of(R, 512)
    for t in range(0, R, tile):
        part = dot(rows_ref[...], basis_ref[:, t : t + tile])
        keep_ref[:, t : t + tile] = part[:top]
        send_ref[:, t : t + tile] = part[top:].astype(BF16)


def both(shape):
    return [sds(shape, F32), sds(shape, BF16)]


def shards(tokens, basis, gate_weight, up_weight, down_weight, *, dp, tensor):
    local, width = tokens.shape
    rows = local * tensor
    ff = gate_weight.shape[1]

    codes, basis = call(
        code_body,
        [sds((local, R), F32), sds(basis.shape, BF16)],
        1,
        tokens,
        basis,
        scratch=[pltpu.VMEM(tokens.shape, BF16), pltpu.SemaphoreType.DMA((PIECES + 1,))],
        fixed=(0, 1),
    )
    codes, send = call(add_two_body, both(codes.shape), WAIT, codes, swap(codes, "dp", 1, dp))
    mask = 2
    while 2 * mask < dp:
        codes, send = call(add_two_body, both(codes.shape), 0.1, codes, swap(send, "dp", mask, dp))
        mask *= 2
    codes = call(add_body, sds(codes.shape, BF16), 0.1, codes, swap(send, "dp", mask, dp))
    mask = 1
    while mask < tensor:
        codes = call(
            join_body, sds((2 * codes.shape[0], R), BF16), 0.1, codes, swap(codes, "tensor", mask, tensor)
        )
        mask *= 2
    restored = call(restore_body, sds((rows, width), BF16), 0.5, codes, basis)

    shares = SHARES if ff % 1024 == 0 else (1, 1)
    spans, at = [], 0
    for share in shares:
        spans.append((at, ff * share // sum(shares)))
        at += spans[-1][1]
    pairs, kept, sums = [], [], []
    for q, (start, span) in enumerate(spans):
        keep, send = call(
            functools.partial(pair_body, start=start),
            both((rows, span)),
            PAIR * span / ff,
            restored,
            gate_weight,
            up_weight,
            *kept[-1:],
            *[send for _, send in sums[-1:]],
        )
        kept.append(keep)
        pairs.append((keep, swap(send, "dp", 1, dp)))
        if q > 0:
            sums.append(call(add_two_body, both((rows, spans[q - 1][1])), SUMS[q - 1], *pairs[q - 1], keep))
    sums.append(call(add_two_body, both((rows, spans[-1][1])), SUMS[-1], *pairs[-1], sums[-1][1]))
    acc = None
    own = None
    for q, ((start, span), (total, send)) in enumerate(zip(spans, sums)):
        mask = 2
        while 2 * mask < dp:
            total, send = call(add_two_body, both(total.shape), 0.1, total, swap(send, "dp", mask, dp))
            mask *= 2
        half = span // 2
        order = [sums[-1][1]] if q == 0 else [acc] if q == 1 else [own]
        own = call(hidden_body, sds((rows, half), BF16), HIDDEN[q], total, swap(send, "dp", mask, dp), *order)
        away = swap(own, "dp", 1, dp)
        time = DOWN * span / ff
        shape = sds((rows, width), F32)
        if start + span < ff:
            body = functools.partial(down_body, start=start, half=half, own=1, away=1, first=acc is None)
            acc = call(body, shape, time, own, away, down_weight, *([] if acc is None else [acc]))
        else:
            body = functools.partial(down_body, start=start, half=half, own=1, away=0, first=False)
            acc = call(body, shape, time / 2, own, down_weight, acc)
            codes, send = call(
                functools.partial(last_body, start=start, half=half),
                [sds((rows // 2, R), F32), sds((rows // 2, R), BF16)],
                1,
                away,
                down_weight,
                acc,
                basis,
                scratch=[pltpu.VMEM((rows, width), BF16)],
            )

    mask = tensor // 2
    while mask > 1:
        top = codes.shape[0] // 2
        codes, send = call(
            half_body, [sds((top, R), F32), sds((top, R), BF16)], 0.1, codes, swap(send, "tensor", mask, tensor)
        )
        mask //= 2
    codes, send = call(add_two_body, both(codes.shape), 0.1, codes, swap(send, "tensor", 1, tensor))
    mask = dp // 2
    while mask > 2:
        codes, send = call(add_two_body, both(codes.shape), 0.1, codes, swap(send, "dp", mask, dp))
        mask //= 2
    codes = call(add_body, sds(codes.shape, F32), 0.1, codes, swap(send, "dp", 2, dp))
    return call(final_body, sds((local, width), BF16), 1, codes, swap(codes, "dp", 1, dp), basis)


SHARES = (2, 1, 1)


def solution(mesh):
    placed = (
        P(("groups", "tensor"), "dp"),
        P("dp", None),
        P("dp", "tensor"),
        P("dp", "tensor"),
        P("tensor", "dp"),
    )
    return jax.shard_map(
        functools.partial(shards, dp=mesh.shape["dp"], tensor=mesh.shape["tensor"]),
        mesh=mesh,
        in_specs=placed,
        out_specs=P(("groups", "tensor"), "dp"),
        check_vma=False,
    )
```

```python
import functools

import jax
import jax.numpy as jnp
from jax import lax
from jax.experimental import pallas as pl
from jax.experimental.pallas import tpu as pltpu
from jax.sharding import PartitionSpec as P

D = 8192
R = 1024
F32 = jnp.float32
BF16 = jnp.bfloat16
LIMIT = 2 * 1024 * 1024
PIECES = 4
WAIT = 30
SUMS = (0.1, 0.1, 0.1)
PAIRS = (3, 1.5, 1.5)
HIDDEN = (3, 0.1, 0.1)
DOWN = (0.1, 0.1, 0.1)
VMEM = pl.BlockSpec(memory_space=pltpu.VMEM)
HBM = pl.BlockSpec(memory_space=pltpu.HBM)
sds = jax.ShapeDtypeStruct


def call(body, out, microseconds, *arrays, scratch=(), fixed=()):
    many = isinstance(out, list)
    return pl.pallas_call(
        body,
        out_shape=out,
        in_specs=[HBM if i in fixed else VMEM for i in range(len(arrays))],
        out_specs=[VMEM] * len(out) if many else VMEM,
        scratch_shapes=list(scratch),
        cost_estimate=pl.CostEstimate(flops=int(microseconds * 1.15e9), bytes_accessed=2**16, transcendentals=0),
        compiler_params=pltpu.CompilerParams(vmem_limit_bytes=LIMIT),
    )(*[pltpu.with_memory_space_constraint(a, pltpu.HBM) if i in fixed else a for i, a in enumerate(arrays)])


def swap(value, axis, mask, size):
    return lax.ppermute(value, axis, [(i, i ^ mask) for i in range(size)])


def tile_of(extent, most):
    tile = most
    while extent % tile:
        tile //= 2
    return tile


def dot(a, b):
    return jnp.dot(a, b, preferred_element_type=F32)


def dot_t(a, b):
    return lax.dot_general(a, b, (((1,), (1,)), ((), ())), preferred_element_type=F32)


def core_index():
    return lax.rem(lax.axis_index("dp"), 2)


def code_body(x_ref, basis_ref, out_ref, held_ref, tokens_ref, sems):
    deep = basis_ref.shape[0] // PIECES
    first = pltpu.make_async_copy(x_ref, tokens_ref, sems.at[PIECES])
    first.start()
    copies = []
    for p in range(PIECES):
        at = pl.ds(p * deep, deep)
        copies.append(pltpu.make_async_copy(basis_ref.at[at], held_ref.at[at], sems.at[p]))
        copies[-1].start()
    first.wait()
    for p in range(PIECES):
        copies[p].wait()
        part = dot(tokens_ref[:, p * deep : (p + 1) * deep], held_ref[p * deep : (p + 1) * deep, :])
        out_ref[...] = part if p == 0 else out_ref[...] + part


def add_body(a_ref, b_ref, *refs, outs=1):
    total = a_ref[...] + b_ref[...].astype(F32)
    for out_ref in refs[-outs:]:
        out_ref[...] = total.astype(out_ref.dtype)


add_two_body = functools.partial(add_body, outs=2)


def half_body(a_ref, b_ref, keep_ref, send_ref):
    top = keep_ref.shape[0]
    keep_ref[...] = a_ref[:top] + b_ref[:top].astype(F32)
    send_ref[...] = (a_ref[top:] + b_ref[top:].astype(F32)).astype(BF16)


def join_body(a_ref, b_ref, out_ref):
    rows = a_ref.shape[0]
    out_ref[:rows] = a_ref[...]
    out_ref[rows:] = b_ref[...]


def hidden_body(a_ref, b_ref, *refs):
    out_ref = refs[-1]
    half = out_ref.shape[1]
    gate = a_ref[:, :half] + b_ref[:, :half].astype(F32)
    up = a_ref[:, half:] + b_ref[:, half:].astype(F32)
    out_ref[...] = (gate / (1 + jnp.exp(-gate)) * up).astype(BF16)


def decode(codes, basis_ref, out_ref):
    factor = (D / R) ** 0.5
    width = basis_ref.shape[0]
    tile = tile_of(width, 512)
    for t in range(0, width, tile):
        out_ref[:, t : t + tile] = (factor * dot_t(codes, basis_ref[t : t + tile, :])).astype(BF16)


def restore_body(codes_ref, basis_ref, out_ref):
    decode(codes_ref[...], basis_ref, out_ref)


def final_body(a_ref, b_ref, basis_ref, out_ref):
    decode((a_ref[...] + b_ref[...]).astype(BF16), basis_ref, out_ref)


def pair_body(x_ref, gate_ref, up_ref, *refs, start):
    keep_ref, send_ref = refs[-2:]
    half = keep_ref.shape[1] // 2
    tile = tile_of(half, 512)
    core = core_index()
    for out_ref, which in ((send_ref, 1 - core), (keep_ref, core)):
        for t in range(0, half, tile):
            at = pl.ds(pl.multiple_of(start + t + which * half, 128), tile)
            out_ref[:, t : t + tile] = dot(x_ref[...], gate_ref[:, at]).astype(out_ref.dtype)
            out_ref[:, half + t : half + t + tile] = dot(x_ref[...], up_ref[:, at]).astype(out_ref.dtype)


def down_body(*refs, parts, first=False):
    h_refs, (weight_ref, *acc, out_ref) = refs[: len(parts)], refs[len(parts) :]
    core = core_index()
    width = out_ref.shape[1]
    tile = tile_of(width, 512)
    for t in range(0, width, tile):
        total = None if first else acc[0][:, t : t + tile]
        for h_ref, (away, start, half) in zip(h_refs, parts):
            at = pl.ds(pl.multiple_of(start + (1 - core if away else core) * half, 16), half)
            part = dot(h_ref[...], weight_ref[at, t : t + tile])
            total = part if total is None else total + part
        out_ref[:, t : t + tile] = total.astype(out_ref.dtype)


def last_body(h_ref, weight_ref, acc_ref, basis_ref, keep_ref, send_ref, rows_ref, *, parts):
    down_body(h_ref, weight_ref, acc_ref, rows_ref, parts=parts)
    top = keep_ref.shape[0]
    tile = tile_of(R, 512)
    for t in range(0, R, tile):
        part = dot(rows_ref[...], basis_ref[:, t : t + tile])
        keep_ref[:, t : t + tile] = part[:top]
        send_ref[:, t : t + tile] = part[top:].astype(BF16)


def both(shape):
    return [sds(shape, F32), sds(shape, BF16)]


def shards(tokens, basis, gate_weight, up_weight, down_weight, *, dp, tensor):
    local, width = tokens.shape
    rows = local * tensor
    ff = gate_weight.shape[1]

    codes, basis = call(
        code_body,
        [sds((local, R), F32), sds(basis.shape, BF16)],
        1,
        tokens,
        basis,
        scratch=[pltpu.VMEM(tokens.shape, BF16), pltpu.SemaphoreType.DMA((PIECES + 1,))],
        fixed=(0, 1),
    )
    codes, send = call(add_two_body, both(codes.shape), WAIT, codes, swap(codes, "dp", 1, dp))
    mask = 2
    while 2 * mask < dp:
        codes, send = call(add_two_body, both(codes.shape), 0.1, codes, swap(send, "dp", mask, dp))
        mask *= 2
    codes = call(add_body, sds(codes.shape, BF16), 0.1, codes, swap(send, "dp", mask, dp))
    mask = 1
    while mask < tensor:
        codes = call(
            join_body, sds((2 * codes.shape[0], R), BF16), 0.1, codes, swap(codes, "tensor", mask, tensor)
        )
        mask *= 2
    restored = call(restore_body, sds((rows, width), BF16), 0.5, codes, basis)

    shares = SHARES if ff % 1024 == 0 else (1, 1)
    spans, at = [], 0
    for share in shares:
        spans.append((at, ff * share // sum(shares)))
        at += spans[-1][1]
    pairs, kept, sums = [], [], []
    for q, (start, span) in enumerate(spans):
        keep, send = call(
            functools.partial(pair_body, start=start),
            both((rows, span)),
            PAIRS[q],
            restored,
            gate_weight,
            up_weight,
            *kept[-1:],
            *[send for _, send in sums[-1:]],
        )
        kept.append(keep)
        pairs.append((keep, swap(send, "dp", 1, dp)))
        if q > 0:
            sums.append(call(add_two_body, both((rows, spans[q - 1][1])), SUMS[q - 1], *pairs[q - 1], keep))
    sums.append(call(add_two_body, both((rows, spans[-1][1])), SUMS[-1], *pairs[-1], sums[-1][1]))
    acc, early, own, late = None, None, None, []
    for q, ((start, span), (total, send)) in enumerate(zip(spans, sums)):
        mask = 2
        while 2 * mask < dp:
            total, send = call(add_two_body, both(total.shape), 0.1, total, swap(send, "dp", mask, dp))
            mask *= 2
        half = span // 2
        order = [sums[-1][1]] if q == 0 else [early] if q == 1 else [own]
        own = call(hidden_body, sds((rows, half), BF16), HIDDEN[q], total, swap(send, "dp", mask, dp), *order)
        away = swap(own, "dp", 1, dp)
        blocks = late + [(own, (0, start, half))]
        body = functools.partial(down_body, parts=tuple(part for _, part in blocks), first=acc is None)
        acc = call(
            body, sds((rows, width), F32), DOWN[q], *[h for h, _ in blocks], down_weight, *([] if acc is None else [acc])
        )
        early = acc if early is None else early
        late = [(away, (1, start, half))]
    ((away, part),) = late
    codes, send = call(
        functools.partial(last_body, parts=(part,)),
        [sds((rows // 2, R), F32), sds((rows // 2, R), BF16)],
        1,
        away,
        down_weight,
        acc,
        basis,
        scratch=[pltpu.VMEM((rows, width), BF16)],
    )

    mask = tensor // 2
    while mask > 1:
        top = codes.shape[0] // 2
        codes, send = call(
            half_body, [sds((top, R), F32), sds((top, R), BF16)], 0.1, codes, swap(send, "tensor", mask, tensor)
        )
        mask //= 2
    codes, send = call(add_two_body, both(codes.shape), 0.1, codes, swap(send, "tensor", 1, tensor))
    mask = dp // 2
    while mask > 2:
        codes, send = call(add_two_body, both(codes.shape), 0.1, codes, swap(send, "dp", mask, dp))
        mask //= 2
    codes = call(add_body, sds(codes.shape, F32), 0.1, codes, swap(send, "dp", 2, dp))
    return call(final_body, sds((local, width), BF16), 1, codes, swap(codes, "dp", 1, dp), basis)


SHARES = (2, 1, 1)


def solution(mesh):
    placed = (
        P(("groups", "tensor"), "dp"),
        P("dp", None),
        P("dp", "tensor"),
        P("dp", "tensor"),
        P("tensor", "dp"),
    )
    return jax.shard_map(
        functools.partial(shards, dp=mesh.shape["dp"], tensor=mesh.shape["tensor"]),
        mesh=mesh,
        in_specs=placed,
        out_specs=P(("groups", "tensor"), "dp"),
        check_vma=False,
    )
```

```python
import functools

import jax
import jax.numpy as jnp
from jax import lax
from jax.experimental import pallas as pl
from jax.experimental.pallas import tpu as pltpu
from jax.sharding import PartitionSpec as P

D = 8192
R = 1024
F32 = jnp.float32
BF16 = jnp.bfloat16
LIMIT = 2 * 1024 * 1024
PIECES = 4
WAIT = 30
TURN = 1
SUMS = (0.1, 1, 0.1)
PAIRS = (3, 1.5, 1.5)
HIDDEN = (2, 0.1, 0.1)
DOWN = (0.1, 0.1, 0.1)
VMEM = pl.BlockSpec(memory_space=pltpu.VMEM)
HBM = pl.BlockSpec(memory_space=pltpu.HBM)
sds = jax.ShapeDtypeStruct


def call(body, out, microseconds, *arrays, scratch=(), fixed=()):
    many = isinstance(out, list)
    return pl.pallas_call(
        body,
        out_shape=out,
        in_specs=[HBM if i in fixed else VMEM for i in range(len(arrays))],
        out_specs=[VMEM] * len(out) if many else VMEM,
        scratch_shapes=list(scratch),
        cost_estimate=pl.CostEstimate(flops=int(microseconds * 1.15e9), bytes_accessed=2**16, transcendentals=0),
        compiler_params=pltpu.CompilerParams(vmem_limit_bytes=LIMIT),
    )(*[pltpu.with_memory_space_constraint(a, pltpu.HBM) if i in fixed else a for i, a in enumerate(arrays)])


def swap(value, axis, mask, size):
    return lax.ppermute(value, axis, [(i, i ^ mask) for i in range(size)])


def tile_of(extent, most):
    tile = most
    while extent % tile:
        tile //= 2
    return tile


def dot(a, b):
    return jnp.dot(a, b, preferred_element_type=F32)


def core_index():
    return lax.rem(lax.axis_index("dp"), 2)


def code_body(x_ref, basis_ref, out_ref, held_ref, tokens_ref, sems):
    deep = basis_ref.shape[0] // PIECES
    first = pltpu.make_async_copy(x_ref, tokens_ref, sems.at[PIECES])
    first.start()
    copies = []
    for p in range(PIECES):
        at = pl.ds(p * deep, deep)
        copies.append(pltpu.make_async_copy(basis_ref.at[at], held_ref.at[at], sems.at[p]))
        copies[-1].start()
    first.wait()
    for p in range(PIECES):
        copies[p].wait()
        part = dot(tokens_ref[:, p * deep : (p + 1) * deep], held_ref[p * deep : (p + 1) * deep, :])
        out_ref[...] = part if p == 0 else out_ref[...] + part


def add_body(a_ref, b_ref, *refs, outs=1):
    total = a_ref[...] + b_ref[...].astype(F32)
    for out_ref in refs[-outs:]:
        out_ref[...] = total.astype(out_ref.dtype)


add_two_body = functools.partial(add_body, outs=2)


def half_body(a_ref, b_ref, keep_ref, send_ref):
    top = keep_ref.shape[0]
    keep_ref[...] = a_ref[:top] + b_ref[:top].astype(F32)
    send_ref[...] = (a_ref[top:] + b_ref[top:].astype(F32)).astype(BF16)


def join_body(a_ref, b_ref, out_ref):
    rows = a_ref.shape[0]
    out_ref[:rows] = a_ref[...]
    out_ref[rows:] = b_ref[...]


def hidden_body(a_ref, b_ref, *refs):
    out_ref = refs[-1]
    half = out_ref.shape[1]
    gate = a_ref[:, :half] + b_ref[:, :half].astype(F32)
    up = a_ref[:, half:] + b_ref[:, half:].astype(F32)
    out_ref[...] = (gate / (1 + jnp.exp(-gate)) * up).astype(BF16)


def turn_body(basis_ref, *refs):
    out_ref = refs[-1]
    width = basis_ref.shape[0]
    tile = tile_of(width, 256)
    for t in range(0, width, tile):
        out_ref[:, t : t + tile] = basis_ref[t : t + tile, :].T


def decode(codes, turned_ref, out_ref):
    factor = (D / R) ** 0.5
    width = turned_ref.shape[1]
    tile = tile_of(width, 512)
    for t in range(0, width, tile):
        out_ref[:, t : t + tile] = (factor * dot(codes, turned_ref[:, t : t + tile])).astype(BF16)


def restore_body(codes_ref, turned_ref, out_ref):
    decode(codes_ref[...], turned_ref, out_ref)


def final_body(a_ref, b_ref, turned_ref, out_ref):
    decode((a_ref[...] + b_ref[...]).astype(BF16), turned_ref, out_ref)


def pair_body(x_ref, gate_ref, up_ref, *refs, start):
    keep_ref, send_ref = refs[-2:]
    half = keep_ref.shape[1] // 2
    tile = tile_of(half, 512)
    core = core_index()
    for out_ref, which in ((send_ref, 1 - core), (keep_ref, core)):
        for t in range(0, half, tile):
            at = pl.ds(pl.multiple_of(start + t + which * half, 128), tile)
            out_ref[:, t : t + tile] = dot(x_ref[...], gate_ref[:, at]).astype(out_ref.dtype)
            out_ref[:, half + t : half + t + tile] = dot(x_ref[...], up_ref[:, at]).astype(out_ref.dtype)


def down_body(*refs, parts, first=False):
    h_refs, (weight_ref, *acc, out_ref) = refs[: len(parts)], refs[len(parts) :]
    core = core_index()
    width = out_ref.shape[1]
    tile = tile_of(width, 512)
    for t in range(0, width, tile):
        total = None if first else acc[0][:, t : t + tile]
        for h_ref, (away, start, half) in zip(h_refs, parts):
            at = pl.ds(pl.multiple_of(start + (1 - core if away else core) * half, 16), half)
            part = dot(h_ref[...], weight_ref[at, t : t + tile])
            total = part if total is None else total + part
        out_ref[:, t : t + tile] = total.astype(out_ref.dtype)


def last_body(h_ref, weight_ref, acc_ref, basis_ref, keep_ref, send_ref, rows_ref, *, parts):
    down_body(h_ref, weight_ref, acc_ref, rows_ref, parts=parts)
    top = keep_ref.shape[0]
    tile = tile_of(R, 512)
    for t in range(0, R, tile):
        part = dot(rows_ref[...], basis_ref[:, t : t + tile])
        keep_ref[:, t : t + tile] = part[:top]
        send_ref[:, t : t + tile] = part[top:].astype(BF16)


def both(shape):
    return [sds(shape, F32), sds(shape, BF16)]


def shards(tokens, basis, gate_weight, up_weight, down_weight, *, dp, tensor):
    local, width = tokens.shape
    rows = local * tensor
    ff = gate_weight.shape[1]

    codes, basis = call(
        code_body,
        [sds((local, R), F32), sds(basis.shape, BF16)],
        1,
        tokens,
        basis,
        scratch=[pltpu.VMEM(tokens.shape, BF16), pltpu.SemaphoreType.DMA((PIECES + 1,))],
        fixed=(0, 1),
    )
    codes, send = call(add_two_body, both(codes.shape), WAIT, codes, swap(codes, "dp", 1, dp))
    mask = 2
    while 2 * mask < dp:
        codes, send = call(add_two_body, both(codes.shape), 0.1, codes, swap(send, "dp", mask, dp))
        mask *= 2
    codes = call(add_body, sds(codes.shape, BF16), 0.1, codes, swap(send, "dp", mask, dp))
    mask = 1
    while mask < tensor:
        if 2 * mask == tensor:
            turned = call(turn_body, sds((R, width), BF16), TURN, basis, codes)
        codes = call(
            join_body, sds((2 * codes.shape[0], R), BF16), 0.1, codes, swap(codes, "tensor", mask, tensor)
        )
        mask *= 2
    restored = call(restore_body, sds((rows, width), BF16), 0.5, codes, turned)

    shares = SHARES if ff % 1024 == 0 else (1, 1)
    spans, at = [], 0
    for share in shares:
        spans.append((at, ff * share // sum(shares)))
        at += spans[-1][1]
    pairs, kept, sums = [], [], []
    for q, (start, span) in enumerate(spans):
        keep, send = call(
            functools.partial(pair_body, start=start),
            both((rows, span)),
            PAIRS[q],
            restored,
            gate_weight,
            up_weight,
            *kept[-1:],
            *[send for _, send in sums[-1:]],
        )
        kept.append(keep)
        pairs.append((keep, swap(send, "dp", 1, dp)))
        if q > 0:
            sums.append(call(add_two_body, both((rows, spans[q - 1][1])), SUMS[q - 1], *pairs[q - 1], keep))
    sums.append(call(add_two_body, both((rows, spans[-1][1])), SUMS[-1], *pairs[-1], sums[-1][1]))
    acc, early, own, late = None, None, None, []
    for q, ((start, span), (total, send)) in enumerate(zip(spans, sums)):
        mask = 2
        while 2 * mask < dp:
            total, send = call(add_two_body, both(total.shape), 0.1, total, swap(send, "dp", mask, dp))
            mask *= 2
        half = span // 2
        order = [sums[-1][1]] if q == 0 else [early] if q == 1 else [own]
        own = call(hidden_body, sds((rows, half), BF16), HIDDEN[q], total, swap(send, "dp", mask, dp), *order)
        away = swap(own, "dp", 1, dp)
        blocks = late + [(own, (0, start, half))]
        body = functools.partial(down_body, parts=tuple(part for _, part in blocks), first=acc is None)
        acc = call(
            body, sds((rows, width), F32), DOWN[q], *[h for h, _ in blocks], down_weight, *([] if acc is None else [acc])
        )
        early = acc if early is None else early
        late = [(away, (1, start, half))]
    ((away, part),) = late
    codes, send = call(
        functools.partial(last_body, parts=(part,)),
        [sds((rows // 2, R), F32), sds((rows // 2, R), BF16)],
        1,
        away,
        down_weight,
        acc,
        basis,
        scratch=[pltpu.VMEM((rows, width), BF16)],
    )

    mask = tensor // 2
    while mask > 1:
        top = codes.shape[0] // 2
        codes, send = call(
            half_body, [sds((top, R), F32), sds((top, R), BF16)], 0.1, codes, swap(send, "tensor", mask, tensor)
        )
        mask //= 2
    codes, send = call(add_two_body, both(codes.shape), 0.1, codes, swap(send, "tensor", 1, tensor))
    mask = dp // 2
    while mask > 2:
        codes, send = call(add_two_body, both(codes.shape), 0.1, codes, swap(send, "dp", mask, dp))
        mask //= 2
    codes = call(add_body, sds(codes.shape, F32), 0.1, codes, swap(send, "dp", 2, dp))
    return call(final_body, sds((local, width), BF16), 1, codes, swap(codes, "dp", 1, dp), turned)


SHARES = (2, 1, 1)


def solution(mesh):
    placed = (
        P(("groups", "tensor"), "dp"),
        P("dp", None),
        P("dp", "tensor"),
        P("dp", "tensor"),
        P("tensor", "dp"),
    )
    return jax.shard_map(
        functools.partial(shards, dp=mesh.shape["dp"], tensor=mesh.shape["tensor"]),
        mesh=mesh,
        in_specs=placed,
        out_specs=P(("groups", "tensor"), "dp"),
        check_vma=False,
    )
```

```python
import functools

import jax
import jax.numpy as jnp
from jax import lax
from jax.experimental import pallas as pl
from jax.experimental.pallas import tpu as pltpu
from jax.sharding import PartitionSpec as P

D = 8192
R = 1024
F32 = jnp.float32
BF16 = jnp.bfloat16
LIMIT = 2 * 1024 * 1024
PIECES = 8
WAIT = 30
TURN = 1
SUMS = (0.1, 1, 0.1, 0.1)
PAIRS = (3, 1.5, 1.5, 0.1)
HIDDEN = (2, 0.1, 0.1, 0.1)
DOWN = (0.1, 0.1, 0.1, 0.1)
VMEM = pl.BlockSpec(memory_space=pltpu.VMEM)
HBM = pl.BlockSpec(memory_space=pltpu.HBM)
sds = jax.ShapeDtypeStruct


def call(body, out, microseconds, *arrays, scratch=(), fixed=()):
    many = isinstance(out, list)
    return pl.pallas_call(
        body,
        out_shape=out,
        in_specs=[HBM if i in fixed else VMEM for i in range(len(arrays))],
        out_specs=[VMEM] * len(out) if many else VMEM,
        scratch_shapes=list(scratch),
        cost_estimate=pl.CostEstimate(flops=int(microseconds * 1.15e9), bytes_accessed=2**16, transcendentals=0),
        compiler_params=pltpu.CompilerParams(vmem_limit_bytes=LIMIT),
    )(*[pltpu.with_memory_space_constraint(a, pltpu.HBM) if i in fixed else a for i, a in enumerate(arrays)])


def swap(value, axis, mask, size):
    return lax.ppermute(value, axis, [(i, i ^ mask) for i in range(size)])


def tile_of(extent, most):
    tile = most
    while extent % tile:
        tile //= 2
    return tile


def dot(a, b):
    return jnp.dot(a, b, preferred_element_type=F32)


def core_index():
    return lax.rem(lax.axis_index("dp"), 2)


def code_body(x_ref, basis_ref, out_ref, held_ref, tokens_ref, sems):
    deep = basis_ref.shape[0] // PIECES
    first = pltpu.make_async_copy(x_ref, tokens_ref, sems.at[PIECES])
    first.start()
    copies = []
    for p in range(PIECES):
        at = pl.ds(p * deep, deep)
        copies.append(pltpu.make_async_copy(basis_ref.at[at], held_ref.at[at], sems.at[p]))
        copies[-1].start()
    first.wait()
    for p in range(PIECES):
        copies[p].wait()
        part = dot(tokens_ref[:, p * deep : (p + 1) * deep], held_ref[p * deep : (p + 1) * deep, :])
        out_ref[...] = part if p == 0 else out_ref[...] + part


def add_body(a_ref, b_ref, *refs, outs=1):
    total = a_ref[...] + b_ref[...].astype(F32)
    for out_ref in refs[-outs:]:
        out_ref[...] = total.astype(out_ref.dtype)


add_two_body = functools.partial(add_body, outs=2)


def half_body(a_ref, b_ref, keep_ref, send_ref):
    top = keep_ref.shape[0]
    keep_ref[...] = a_ref[:top] + b_ref[:top].astype(F32)
    send_ref[...] = (a_ref[top:] + b_ref[top:].astype(F32)).astype(BF16)


def join_body(a_ref, b_ref, out_ref):
    rows = a_ref.shape[0]
    out_ref[:rows] = a_ref[...]
    out_ref[rows:] = b_ref[...]


def hidden_body(a_ref, b_ref, *refs):
    out_ref = refs[-1]
    half = out_ref.shape[1]
    gate = a_ref[:, :half] + b_ref[:, :half].astype(F32)
    up = a_ref[:, half:] + b_ref[:, half:].astype(F32)
    out_ref[...] = (gate / (1 + jnp.exp(-gate)) * up).astype(BF16)


def turn_body(basis_ref, *refs):
    out_ref = refs[-1]
    width = basis_ref.shape[0]
    tile = tile_of(width, 256)
    for t in range(0, width, tile):
        out_ref[:, t : t + tile] = basis_ref[t : t + tile, :].T


def decode(codes, turned_ref, out_ref):
    factor = (D / R) ** 0.5
    width = turned_ref.shape[1]
    tile = tile_of(width, 512)
    for t in range(0, width, tile):
        out_ref[:, t : t + tile] = (factor * dot(codes, turned_ref[:, t : t + tile])).astype(BF16)


def restore_body(codes_ref, turned_ref, out_ref):
    decode(codes_ref[...], turned_ref, out_ref)


def final_body(a_ref, b_ref, turned_ref, out_ref):
    decode((a_ref[...] + b_ref[...]).astype(BF16), turned_ref, out_ref)


def pair_body(x_ref, gate_ref, up_ref, *refs, start):
    keep_ref, send_ref = refs[-2:]
    half = keep_ref.shape[1] // 2
    tile = tile_of(half, 512)
    core = core_index()
    for out_ref, which in ((send_ref, 1 - core), (keep_ref, core)):
        for t in range(0, half, tile):
            at = pl.ds(pl.multiple_of(start + t + which * half, 128), tile)
            out_ref[:, t : t + tile] = dot(x_ref[...], gate_ref[:, at]).astype(out_ref.dtype)
            out_ref[:, half + t : half + t + tile] = dot(x_ref[...], up_ref[:, at]).astype(out_ref.dtype)


def down_body(*refs, parts, first=False):
    h_refs, (weight_ref, *acc, out_ref) = refs[: len(parts)], refs[len(parts) :]
    core = core_index()
    width = out_ref.shape[1]
    tile = tile_of(width, 512)
    for t in range(0, width, tile):
        total = None if first else acc[0][:, t : t + tile]
        for h_ref, (away, start, half) in zip(h_refs, parts):
            at = pl.ds(pl.multiple_of(start + (1 - core if away else core) * half, 16), half)
            part = dot(h_ref[...], weight_ref[at, t : t + tile])
            total = part if total is None else total + part
        out_ref[:, t : t + tile] = total.astype(out_ref.dtype)


def last_body(h_ref, weight_ref, acc_ref, basis_ref, keep_ref, send_ref, rows_ref, *, parts):
    down_body(h_ref, weight_ref, acc_ref, rows_ref, parts=parts)
    top = keep_ref.shape[0]
    tile = tile_of(R, 512)
    for t in range(0, R, tile):
        part = dot(rows_ref[...], basis_ref[:, t : t + tile])
        keep_ref[:, t : t + tile] = part[:top]
        send_ref[:, t : t + tile] = part[top:].astype(BF16)


def both(shape):
    return [sds(shape, F32), sds(shape, BF16)]


def shards(tokens, basis, gate_weight, up_weight, down_weight, *, dp, tensor):
    local, width = tokens.shape
    rows = local * tensor
    ff = gate_weight.shape[1]

    codes, basis = call(
        code_body,
        [sds((local, R), F32), sds(basis.shape, BF16)],
        1,
        tokens,
        basis,
        scratch=[pltpu.VMEM(tokens.shape, BF16), pltpu.SemaphoreType.DMA((PIECES + 1,))],
        fixed=(0, 1),
    )
    codes, send = call(add_two_body, both(codes.shape), WAIT, codes, swap(codes, "dp", 1, dp))
    mask = 2
    while 2 * mask < dp:
        codes, send = call(add_two_body, both(codes.shape), 0.1, codes, swap(send, "dp", mask, dp))
        mask *= 2
    codes = call(add_body, sds(codes.shape, BF16), 0.1, codes, swap(send, "dp", mask, dp))
    mask = 1
    while mask < tensor:
        if 2 * mask == tensor:
            turned = call(turn_body, sds((R, width), BF16), TURN, basis, codes)
        codes = call(
            join_body, sds((2 * codes.shape[0], R), BF16), 0.1, codes, swap(codes, "tensor", mask, tensor)
        )
        mask *= 2
    restored = call(restore_body, sds((rows, width), BF16), 0.5, codes, turned)

    shares = SHARES if ff % (256 * sum(SHARES)) == 0 else (1, 1)
    spans, at = [], 0
    for share in shares:
        spans.append((at, ff * share // sum(shares)))
        at += spans[-1][1]
    pairs, kept, sums = [], [], []
    for q, (start, span) in enumerate(spans):
        keep, send = call(
            functools.partial(pair_body, start=start),
            both((rows, span)),
            PAIRS[q],
            restored,
            gate_weight,
            up_weight,
            *kept[-1:],
            *[send for _, send in sums[-1:]],
        )
        kept.append(keep)
        pairs.append((keep, swap(send, "dp", 1, dp)))
        if q > 0:
            sums.append(call(add_two_body, both((rows, spans[q - 1][1])), SUMS[q - 1], *pairs[q - 1], keep))
    sums.append(call(add_two_body, both((rows, spans[-1][1])), SUMS[len(spans) - 1], *pairs[-1], sums[-1][1]))
    acc, late = None, []
    for q, ((start, span), (total, send)) in enumerate(zip(spans, sums)):
        mask = 2
        while 2 * mask < dp:
            total, send = call(add_two_body, both(total.shape), 0.1, total, swap(send, "dp", mask, dp))
            mask *= 2
        half = span // 2
        order = [sums[-1][1]] if q == 0 else [acc]
        own = call(hidden_body, sds((rows, half), BF16), HIDDEN[q], total, swap(send, "dp", mask, dp), *order)
        away = swap(own, "dp", 1, dp)
        blocks = late + [(own, (0, start, half))]
        body = functools.partial(down_body, parts=tuple(part for _, part in blocks), first=acc is None)
        acc = call(
            body, sds((rows, width), F32), DOWN[q], *[h for h, _ in blocks], down_weight, *([] if acc is None else [acc])
        )
        late = [(away, (1, start, half))]
    ((away, part),) = late
    codes, send = call(
        functools.partial(last_body, parts=(part,)),
        [sds((rows // 2, R), F32), sds((rows // 2, R), BF16)],
        1,
        away,
        down_weight,
        acc,
        basis,
        scratch=[pltpu.VMEM((rows, width), BF16)],
    )

    mask = tensor // 2
    while mask > 1:
        top = codes.shape[0] // 2
        codes, send = call(
            half_body, [sds((top, R), F32), sds((top, R), BF16)], 0.1, codes, swap(send, "tensor", mask, tensor)
        )
        mask //= 2
    codes, send = call(add_two_body, both(codes.shape), 0.1, codes, swap(send, "tensor", 1, tensor))
    mask = dp // 2
    while mask > 2:
        codes, send = call(add_two_body, both(codes.shape), 0.1, codes, swap(send, "dp", mask, dp))
        mask //= 2
    codes = call(add_body, sds(codes.shape, F32), 0.1, codes, swap(send, "dp", 2, dp))
    return call(final_body, sds((local, width), BF16), 1, codes, swap(codes, "dp", 1, dp), turned)


SHARES = (3, 3, 2)


def solution(mesh):
    placed = (
        P(("groups", "tensor"), "dp"),
        P("dp", None),
        P("dp", "tensor"),
        P("dp", "tensor"),
        P("tensor", "dp"),
    )
    return jax.shard_map(
        functools.partial(shards, dp=mesh.shape["dp"], tensor=mesh.shape["tensor"]),
        mesh=mesh,
        in_specs=placed,
        out_specs=P(("groups", "tensor"), "dp"),
        check_vma=False,
    )
```

```python
import functools

import jax
import jax.numpy as jnp
from jax import lax
from jax.experimental import pallas as pl
from jax.experimental.pallas import tpu as pltpu
from jax.sharding import PartitionSpec as P

D = 8192
R = 1024
F32 = jnp.float32
BF16 = jnp.bfloat16
LIMIT = 2 * 1024 * 1024
PIECES = 8
WAIT = 30
TURN = 1
SUMS = (0.1, 1, 0.1, 0.1)
PAIRS = (3, 1.5, 1.5, 0.1)
HIDDEN = (2, 0.1, 0.1, 0.1)
DOWN = (0.1, 0.1, 0.1, 0.1)
VMEM = pl.BlockSpec(memory_space=pltpu.VMEM)
HBM = pl.BlockSpec(memory_space=pltpu.HBM)
sds = jax.ShapeDtypeStruct


def call(body, out, microseconds, *arrays, scratch=(), fixed=()):
    many = isinstance(out, list)
    return pl.pallas_call(
        body,
        out_shape=out,
        in_specs=[HBM if i in fixed else VMEM for i in range(len(arrays))],
        out_specs=[VMEM] * len(out) if many else VMEM,
        scratch_shapes=list(scratch),
        cost_estimate=pl.CostEstimate(flops=int(microseconds * 1.15e9), bytes_accessed=2**16, transcendentals=0),
        compiler_params=pltpu.CompilerParams(vmem_limit_bytes=LIMIT),
    )(*[pltpu.with_memory_space_constraint(a, pltpu.HBM) if i in fixed else a for i, a in enumerate(arrays)])


def swap(value, axis, mask, size):
    return lax.ppermute(value, axis, [(i, i ^ mask) for i in range(size)])


def tile_of(extent, most):
    tile = most
    while extent % tile:
        tile //= 2
    return tile


def dot(a, b):
    return jnp.dot(a, b, preferred_element_type=F32)


def core_index():
    return lax.rem(lax.axis_index("dp"), 2)


def code_body(x_ref, basis_ref, out_ref, held_ref, tokens_ref, sems):
    deep = basis_ref.shape[0] // PIECES
    first = pltpu.make_async_copy(x_ref, tokens_ref, sems.at[PIECES])
    first.start()
    copies = []
    for p in range(PIECES):
        at = pl.ds(p * deep, deep)
        copies.append(pltpu.make_async_copy(basis_ref.at[at], held_ref.at[at], sems.at[p]))
        copies[-1].start()
    first.wait()
    for p in range(PIECES):
        copies[p].wait()
        part = dot(tokens_ref[:, p * deep : (p + 1) * deep], held_ref[p * deep : (p + 1) * deep, :])
        out_ref[...] = part if p == 0 else out_ref[...] + part


def add_body(a_ref, b_ref, *refs, outs=1):
    total = a_ref[...] + b_ref[...].astype(F32)
    for out_ref in refs[-outs:]:
        out_ref[...] = total.astype(out_ref.dtype)


add_two_body = functools.partial(add_body, outs=2)


def half_body(a_ref, b_ref, keep_ref, send_ref):
    top = keep_ref.shape[0]
    keep_ref[...] = a_ref[:top] + b_ref[:top].astype(F32)
    send_ref[...] = (a_ref[top:] + b_ref[top:].astype(F32)).astype(BF16)


def join_body(a_ref, b_ref, out_ref):
    rows = a_ref.shape[0]
    out_ref[:rows] = a_ref[...]
    out_ref[rows:] = b_ref[...]


def hidden_body(a_ref, b_ref, *refs):
    out_ref = refs[-1]
    half = out_ref.shape[1]
    gate = a_ref[:, :half] + b_ref[:, :half].astype(F32)
    up = a_ref[:, half:] + b_ref[:, half:].astype(F32)
    out_ref[...] = (gate / (1 + jnp.exp(-gate)) * up).astype(BF16)


def turn_body(basis_ref, *refs):
    out_ref = refs[-1]
    width = basis_ref.shape[0]
    tile = tile_of(width, 256)
    for t in range(0, width, tile):
        out_ref[:, t : t + tile] = basis_ref[t : t + tile, :].T


def decode(codes, turned_ref, out_ref):
    factor = (D / R) ** 0.5
    width = turned_ref.shape[1]
    tile = tile_of(width, 512)
    for t in range(0, width, tile):
        out_ref[:, t : t + tile] = (factor * dot(codes, turned_ref[:, t : t + tile])).astype(BF16)


def restore_body(codes_ref, turned_ref, out_ref):
    decode(codes_ref[...], turned_ref, out_ref)


def final_body(a_ref, b_ref, turned_ref, out_ref):
    decode((a_ref[...] + b_ref[...]).astype(BF16), turned_ref, out_ref)


def pair_body(x_ref, gate_ref, up_ref, *refs, start):
    keep_ref, send_ref = refs[-2:]
    half = keep_ref.shape[1] // 2
    tile = tile_of(half, 512)
    core = core_index()
    for out_ref, which in ((send_ref, 1 - core), (keep_ref, core)):
        for t in range(0, half, tile):
            at = pl.ds(pl.multiple_of(start + t + which * half, 128), tile)
            out_ref[:, t : t + tile] = dot(x_ref[...], gate_ref[:, at]).astype(out_ref.dtype)
            out_ref[:, half + t : half + t + tile] = dot(x_ref[...], up_ref[:, at]).astype(out_ref.dtype)


def down_body(*refs, parts, first=False):
    h_refs, (weight_ref, *acc, out_ref) = refs[: len(parts)], refs[len(parts) :]
    core = core_index()
    width = out_ref.shape[1]
    tile = tile_of(width, 512)
    for t in range(0, width, tile):
        total = None if first else acc[0][:, t : t + tile]
        for h_ref, (away, start, half) in zip(h_refs, parts):
            at = pl.ds(pl.multiple_of(start + (1 - core if away else core) * half, 16), half)
            part = dot(h_ref[...], weight_ref[at, t : t + tile])
            total = part if total is None else total + part
        out_ref[:, t : t + tile] = total.astype(out_ref.dtype)


def last_body(h_ref, weight_ref, acc_ref, basis_ref, keep_ref, send_ref, rows_ref, *, parts):
    down_body(h_ref, weight_ref, acc_ref, rows_ref, parts=parts)
    top = keep_ref.shape[0]
    tile = tile_of(R, 512)
    for t in range(0, R, tile):
        part = dot(rows_ref[...], basis_ref[:, t : t + tile])
        keep_ref[:, t : t + tile] = part[:top]
        send_ref[:, t : t + tile] = part[top:].astype(BF16)


def both(shape):
    return [sds(shape, F32), sds(shape, BF16)]


def shards(tokens, basis, gate_weight, up_weight, down_weight, *, dp, tensor):
    local, width = tokens.shape
    rows = local * tensor
    ff = gate_weight.shape[1]

    codes, basis = call(
        code_body,
        [sds((local, R), F32), sds(basis.shape, BF16)],
        1,
        tokens,
        basis,
        scratch=[pltpu.VMEM(tokens.shape, BF16), pltpu.SemaphoreType.DMA((PIECES + 1,))],
        fixed=(0, 1),
    )
    codes, send = call(add_two_body, both(codes.shape), WAIT, codes, swap(codes, "dp", 1, dp))
    mask = 2
    while 2 * mask < dp:
        codes, send = call(add_two_body, both(codes.shape), 0.1, codes, swap(send, "dp", mask, dp))
        mask *= 2
    codes = call(add_body, sds(codes.shape, BF16), 0.1, codes, swap(send, "dp", mask, dp))
    mask = 1
    while mask < tensor:
        if 2 * mask == tensor:
            turned = call(turn_body, sds((R, width), BF16), TURN, basis, codes)
        codes = call(
            join_body, sds((2 * codes.shape[0], R), BF16), 0.1, codes, swap(codes, "tensor", mask, tensor)
        )
        mask *= 2
    restored = call(restore_body, sds((rows, width), BF16), 0.5, codes, turned)

    shares = SHARES if ff % (256 * sum(SHARES)) == 0 else (1, 1)
    spans, at = [], 0
    for share in shares:
        spans.append((at, ff * share // sum(shares)))
        at += spans[-1][1]
    pairs, kept, sums = [], [], []
    for q, (start, span) in enumerate(spans):
        keep, send = call(
            functools.partial(pair_body, start=start),
            both((rows, span)),
            PAIRS[q],
            restored,
            gate_weight,
            up_weight,
            *kept[-1:],
            *[send for _, send in sums[-1:]],
        )
        kept.append(keep)
        pairs.append((keep, swap(send, "dp", 1, dp)))
        if q > 0:
            sums.append(call(add_two_body, both((rows, spans[q - 1][1])), SUMS[q - 1], *pairs[q - 1], keep))
    sums.append(call(add_two_body, both((rows, spans[-1][1])), SUMS[len(spans) - 1], *pairs[-1], sums[-1][1]))
    acc, late = None, []
    for q, ((start, span), (total, send)) in enumerate(zip(spans, sums)):
        mask = 2
        while 2 * mask < dp:
            total, send = call(add_two_body, both(total.shape), 0.1, total, swap(send, "dp", mask, dp))
            mask *= 2
        half = span // 2
        order = [sums[-1][1]] if q == 0 else [acc]
        own = call(hidden_body, sds((rows, half), BF16), HIDDEN[q], total, swap(send, "dp", mask, dp), *order)
        away = swap(own, "dp", 1, dp)
        blocks = late + [(own, (0, start, half))]
        body = functools.partial(down_body, parts=tuple(part for _, part in blocks), first=acc is None)
        acc = call(
            body, sds((rows, width), F32), DOWN[q], *[h for h, _ in blocks], down_weight, *([] if acc is None else [acc])
        )
        late = [(away, (1, start, half))]
    ((away, part),) = late
    codes, send = call(
        functools.partial(last_body, parts=(part,)),
        [sds((rows // 2, R), F32), sds((rows // 2, R), BF16)],
        1,
        away,
        down_weight,
        acc,
        basis,
        scratch=[pltpu.VMEM((rows, width), BF16)],
    )

    mask = tensor // 2
    while mask > 1:
        top = codes.shape[0] // 2
        codes, send = call(
            half_body, [sds((top, R), F32), sds((top, R), BF16)], 0.1, codes, swap(send, "tensor", mask, tensor)
        )
        mask //= 2
    codes, send = call(add_two_body, both(codes.shape), 0.1, codes, swap(send, "tensor", 1, tensor))
    mask = dp // 2
    while mask > 2:
        codes, send = call(add_two_body, both(codes.shape), 0.1, codes, swap(send, "dp", mask, dp))
        mask //= 2
    codes = call(add_body, sds(codes.shape, F32), 0.1, codes, swap(send, "dp", 2, dp))
    return call(final_body, sds((local, width), BF16), 1, codes, swap(codes, "dp", 1, dp), turned)


SHARES = (4, 1, 3)


def solution(mesh):
    placed = (
        P(("groups", "tensor"), "dp"),
        P("dp", None),
        P("dp", "tensor"),
        P("dp", "tensor"),
        P("tensor", "dp"),
    )
    return jax.shard_map(
        functools.partial(shards, dp=mesh.shape["dp"], tensor=mesh.shape["tensor"]),
        mesh=mesh,
        in_specs=placed,
        out_specs=P(("groups", "tensor"), "dp"),
        check_vma=False,
    )
```

```python
import functools

import jax
import jax.numpy as jnp
from jax import lax
from jax.experimental import pallas as pl
from jax.experimental.pallas import tpu as pltpu
from jax.sharding import PartitionSpec as P

D = 8192
R = 1024
F32 = jnp.float32
BF16 = jnp.bfloat16
LIMIT = 2 * 1024 * 1024
PIECES = 8
WAIT = 30
TURN = 1
SUMS = (0.1, 1, 0.1, 0.1)
PAIRS = (3, 1.5, 1.5, 0.1)
HIDDEN = (2, 0.1, 0.1, 0.1)
DOWN = (0.1, 0.1, 0.1, 0.1)
VMEM = pl.BlockSpec(memory_space=pltpu.VMEM)
HBM = pl.BlockSpec(memory_space=pltpu.HBM)
sds = jax.ShapeDtypeStruct


def call(body, out, microseconds, *arrays, scratch=(), fixed=()):
    many = isinstance(out, list)
    return pl.pallas_call(
        body,
        out_shape=out,
        in_specs=[HBM if i in fixed else VMEM for i in range(len(arrays))],
        out_specs=[VMEM] * len(out) if many else VMEM,
        scratch_shapes=list(scratch),
        cost_estimate=pl.CostEstimate(flops=int(microseconds * 1.15e9), bytes_accessed=2**16, transcendentals=0),
        compiler_params=pltpu.CompilerParams(vmem_limit_bytes=LIMIT),
    )(*[pltpu.with_memory_space_constraint(a, pltpu.HBM) if i in fixed else a for i, a in enumerate(arrays)])


def swap(value, axis, mask, size):
    return lax.ppermute(value, axis, [(i, i ^ mask) for i in range(size)])


def tile_of(extent, most):
    tile = most
    while extent % tile:
        tile //= 2
    return tile


def dot(a, b):
    return jnp.dot(a, b, preferred_element_type=F32)


def core_index():
    return lax.rem(lax.axis_index("dp"), 2)


def code_body(x_ref, basis_ref, out_ref, held_ref, tokens_ref, sems):
    deep = basis_ref.shape[0] // PIECES
    first = pltpu.make_async_copy(x_ref, tokens_ref, sems.at[PIECES])
    first.start()
    copies = []
    for p in range(PIECES):
        at = pl.ds(p * deep, deep)
        copies.append(pltpu.make_async_copy(basis_ref.at[at], held_ref.at[at], sems.at[p]))
        copies[-1].start()
    first.wait()
    for p in range(PIECES):
        copies[p].wait()
        part = dot(tokens_ref[:, p * deep : (p + 1) * deep], held_ref[p * deep : (p + 1) * deep, :])
        out_ref[...] = part if p == 0 else out_ref[...] + part


def add_body(a_ref, b_ref, *refs, outs=1):
    total = a_ref[...] + b_ref[...].astype(F32)
    for out_ref in refs[-outs:]:
        out_ref[...] = total.astype(out_ref.dtype)


add_two_body = functools.partial(add_body, outs=2)


def half_body(a_ref, b_ref, keep_ref, send_ref):
    top = keep_ref.shape[0]
    keep_ref[...] = a_ref[:top] + b_ref[:top].astype(F32)
    send_ref[...] = (a_ref[top:] + b_ref[top:].astype(F32)).astype(BF16)


def join_body(a_ref, b_ref, out_ref):
    rows = a_ref.shape[0]
    out_ref[:rows] = a_ref[...]
    out_ref[rows:] = b_ref[...]


def hidden_body(a_ref, b_ref, *refs):
    out_ref = refs[-1]
    half = out_ref.shape[1]
    gate = a_ref[:, :half] + b_ref[:, :half].astype(F32)
    up = a_ref[:, half:] + b_ref[:, half:].astype(F32)
    out_ref[...] = (gate / (1 + jnp.exp(-gate)) * up).astype(BF16)


def turn_body(basis_ref, *refs):
    out_ref = refs[-1]
    width = basis_ref.shape[0]
    tile = tile_of(width, 256)
    for t in range(0, width, tile):
        out_ref[:, t : t + tile] = basis_ref[t : t + tile, :].T


def decode(codes, turned_ref, out_ref):
    factor = (D / R) ** 0.5
    width = turned_ref.shape[1]
    tile = tile_of(width, 512)
    for t in range(0, width, tile):
        out_ref[:, t : t + tile] = (factor * dot(codes, turned_ref[:, t : t + tile])).astype(BF16)


def restore_body(codes_ref, turned_ref, out_ref):
    decode(codes_ref[...], turned_ref, out_ref)


def final_body(a_ref, b_ref, turned_ref, out_ref):
    decode((a_ref[...] + b_ref[...]).astype(BF16), turned_ref, out_ref)


def pair_body(x_ref, gate_ref, up_ref, *refs, start):
    keep_ref, send_ref = refs[-2:]
    half = keep_ref.shape[1] // 2
    tile = tile_of(half, 512)
    core = core_index()
    for out_ref, which in ((send_ref, 1 - core), (keep_ref, core)):
        for t in range(0, half, tile):
            at = pl.ds(pl.multiple_of(start + t + which * half, 128), tile)
            out_ref[:, t : t + tile] = dot(x_ref[...], gate_ref[:, at]).astype(out_ref.dtype)
            out_ref[:, half + t : half + t + tile] = dot(x_ref[...], up_ref[:, at]).astype(out_ref.dtype)


def down_body(*refs, parts, first=False):
    h_refs, (weight_ref, *acc, out_ref) = refs[: len(parts)], refs[len(parts) :]
    core = core_index()
    width = out_ref.shape[1]
    tile = tile_of(width, 512)
    for t in range(0, width, tile):
        total = None if first else acc[0][:, t : t + tile]
        for h_ref, (away, start, half) in zip(h_refs, parts):
            at = pl.ds(pl.multiple_of(start + (1 - core if away else core) * half, 16), half)
            part = dot(h_ref[...], weight_ref[at, t : t + tile])
            total = part if total is None else total + part
        out_ref[:, t : t + tile] = total.astype(out_ref.dtype)


def last_body(h_ref, weight_ref, acc_ref, basis_ref, keep_ref, send_ref, rows_ref, *, parts):
    down_body(h_ref, weight_ref, acc_ref, rows_ref, parts=parts)
    top = keep_ref.shape[0]
    tile = tile_of(R, 512)
    for t in range(0, R, tile):
        part = dot(rows_ref[...], basis_ref[:, t : t + tile])
        keep_ref[:, t : t + tile] = part[:top]
        send_ref[:, t : t + tile] = part[top:].astype(BF16)


def both(shape):
    return [sds(shape, F32), sds(shape, BF16)]


def shards(tokens, basis, gate_weight, up_weight, down_weight, *, dp, tensor):
    local, width = tokens.shape
    rows = local * tensor
    ff = gate_weight.shape[1]

    codes, basis = call(
        code_body,
        [sds((local, R), F32), sds(basis.shape, BF16)],
        1,
        tokens,
        basis,
        scratch=[pltpu.VMEM(tokens.shape, BF16), pltpu.SemaphoreType.DMA((PIECES + 1,))],
        fixed=(0, 1),
    )
    codes, send = call(add_two_body, both(codes.shape), WAIT, codes, swap(codes, "dp", 1, dp))
    mask = 2
    while 2 * mask < dp:
        codes, send = call(add_two_body, both(codes.shape), 0.1, codes, swap(send, "dp", mask, dp))
        mask *= 2
    codes = call(add_body, sds(codes.shape, BF16), 0.1, codes, swap(send, "dp", mask, dp))
    mask = 1
    while mask < tensor:
        if 2 * mask == tensor:
            turned = call(turn_body, sds((R, width), BF16), TURN, basis, codes)
        codes = call(
            join_body, sds((2 * codes.shape[0], R), BF16), 0.1, codes, swap(codes, "tensor", mask, tensor)
        )
        mask *= 2
    restored = call(restore_body, sds((rows, width), BF16), 0.5, codes, turned)

    shares = SHARES if ff % (256 * sum(SHARES)) == 0 else (1, 1)
    spans, at = [], 0
    for share in shares:
        spans.append((at, ff * share // sum(shares)))
        at += spans[-1][1]
    pairs, kept, sums = [], [], []
    for q, (start, span) in enumerate(spans):
        keep, send = call(
            functools.partial(pair_body, start=start),
            both((rows, span)),
            PAIRS[q],
            restored,
            gate_weight,
            up_weight,
            *kept[-1:],
            *[send for _, send in sums[-1:]],
        )
        kept.append(keep)
        pairs.append((keep, swap(send, "dp", 1, dp)))
        if q > 0:
            sums.append(call(add_two_body, both((rows, spans[q - 1][1])), SUMS[q - 1], *pairs[q - 1], keep))
    sums.append(call(add_two_body, both((rows, spans[-1][1])), SUMS[len(spans) - 1], *pairs[-1], sums[-1][1]))
    acc, late = None, []
    for q, ((start, span), (total, send)) in enumerate(zip(spans, sums)):
        mask = 2
        while 2 * mask < dp:
            total, send = call(add_two_body, both(total.shape), 0.1, total, swap(send, "dp", mask, dp))
            mask *= 2
        half = span // 2
        order = [sums[-1][1]] if q == 0 else [acc]
        own = call(hidden_body, sds((rows, half), BF16), HIDDEN[q], total, swap(send, "dp", mask, dp), *order)
        away = swap(own, "dp", 1, dp)
        blocks = late + [(own, (0, start, half))]
        body = functools.partial(down_body, parts=tuple(part for _, part in blocks), first=acc is None)
        acc = call(
            body, sds((rows, width), F32), DOWN[q], *[h for h, _ in blocks], down_weight, *([] if acc is None else [acc])
        )
        late = [(away, (1, start, half))]
    ((away, part),) = late
    codes, send = call(
        functools.partial(last_body, parts=(part,)),
        [sds((rows // 2, R), F32), sds((rows // 2, R), BF16)],
        1,
        away,
        down_weight,
        acc,
        basis,
        scratch=[pltpu.VMEM((rows, width), BF16)],
    )

    mask = tensor // 2
    while mask > 1:
        top = codes.shape[0] // 2
        codes, send = call(
            half_body, [sds((top, R), F32), sds((top, R), BF16)], 0.1, codes, swap(send, "tensor", mask, tensor)
        )
        mask //= 2
    codes, send = call(add_two_body, both(codes.shape), 0.1, codes, swap(send, "tensor", 1, tensor))
    mask = dp // 2
    while mask > 2:
        codes, send = call(add_two_body, both(codes.shape), 0.1, codes, swap(send, "dp", mask, dp))
        mask //= 2
    codes = call(add_body, sds(codes.shape, F32), 0.1, codes, swap(send, "dp", 2, dp))
    return call(final_body, sds((local, width), BF16), 1, codes, swap(codes, "dp", 1, dp), turned)


SHARES = (4, 2, 2)


def solution(mesh):
    placed = (
        P(("groups", "tensor"), "dp"),
        P("dp", None),
        P("dp", "tensor"),
        P("dp", "tensor"),
        P("tensor", "dp"),
    )
    return jax.shard_map(
        functools.partial(shards, dp=mesh.shape["dp"], tensor=mesh.shape["tensor"]),
        mesh=mesh,
        in_specs=placed,
        out_specs=P(("groups", "tensor"), "dp"),
        check_vma=False,
    )
```

```python
import functools

import jax
import jax.numpy as jnp
from jax import lax
from jax.experimental import pallas as pl
from jax.experimental.pallas import tpu as pltpu
from jax.sharding import PartitionSpec as P

D = 8192
R = 1024
F32 = jnp.float32
BF16 = jnp.bfloat16
LIMIT = 2 * 1024 * 1024
PIECES = 8
WAIT = 30
TURN = 1
SUMS = (0.1, 1, 0.1)
PAIRS = (3, 1.5, 1.5)
HIDDEN = (2, 0.1, 0.1)
DOWN = (0.1, 0.1, 0.1)
VMEM = pl.BlockSpec(memory_space=pltpu.VMEM)
HBM = pl.BlockSpec(memory_space=pltpu.HBM)
sds = jax.ShapeDtypeStruct


def call(body, out, microseconds, *arrays, scratch=(), fixed=()):
    many = isinstance(out, list)
    return pl.pallas_call(
        body,
        out_shape=out,
        in_specs=[HBM if i in fixed else VMEM for i in range(len(arrays))],
        out_specs=[VMEM] * len(out) if many else VMEM,
        scratch_shapes=list(scratch),
        cost_estimate=pl.CostEstimate(flops=int(microseconds * 1.15e9), bytes_accessed=2**16, transcendentals=0),
        compiler_params=pltpu.CompilerParams(vmem_limit_bytes=LIMIT),
    )(*[pltpu.with_memory_space_constraint(a, pltpu.HBM) if i in fixed else a for i, a in enumerate(arrays)])


def swap(value, axis, mask, size):
    return lax.ppermute(value, axis, [(i, i ^ mask) for i in range(size)])


def tile_of(extent, most):
    tile = most
    while extent % tile:
        tile //= 2
    return tile


def dot(a, b):
    return jnp.dot(a, b, preferred_element_type=F32)


def core_index():
    return lax.rem(lax.axis_index("dp"), 2)


def code_body(x_ref, basis_ref, out_ref, held_ref, tokens_ref, sems):
    deep = basis_ref.shape[0] // PIECES
    first = pltpu.make_async_copy(x_ref, tokens_ref, sems.at[PIECES])
    first.start()
    copies = []
    for p in range(PIECES):
        at = pl.ds(p * deep, deep)
        copies.append(pltpu.make_async_copy(basis_ref.at[at], held_ref.at[at], sems.at[p]))
        copies[-1].start()
    first.wait()
    for p in range(PIECES):
        copies[p].wait()
        part = dot(tokens_ref[:, p * deep : (p + 1) * deep], held_ref[p * deep : (p + 1) * deep, :])
        out_ref[...] = part if p == 0 else out_ref[...] + part


def add_body(a_ref, b_ref, *refs, outs=1):
    total = a_ref[...] + b_ref[...].astype(F32)
    for out_ref in refs[-outs:]:
        out_ref[...] = total.astype(out_ref.dtype)


add_two_body = functools.partial(add_body, outs=2)


def half_body(a_ref, b_ref, keep_ref, send_ref):
    top = keep_ref.shape[0]
    keep_ref[...] = a_ref[:top] + b_ref[:top].astype(F32)
    send_ref[...] = (a_ref[top:] + b_ref[top:].astype(F32)).astype(BF16)


def join_body(a_ref, b_ref, out_ref):
    rows = a_ref.shape[0]
    out_ref[:rows] = a_ref[...]
    out_ref[rows:] = b_ref[...]


def hidden_body(a_ref, b_ref, *refs):
    out_ref = refs[-1]
    half = out_ref.shape[1]
    gate = a_ref[:, :half] + b_ref[:, :half].astype(F32)
    up = a_ref[:, half:] + b_ref[:, half:].astype(F32)
    out_ref[...] = (gate / (1 + jnp.exp(-gate)) * up).astype(BF16)


def turn_body(basis_ref, *refs):
    out_ref = refs[-1]
    width = basis_ref.shape[0]
    tile = tile_of(width, 256)
    for t in range(0, width, tile):
        out_ref[:, t : t + tile] = basis_ref[t : t + tile, :].T


def decode(codes, turned_ref, out_ref):
    factor = (D / R) ** 0.5
    width = turned_ref.shape[1]
    tile = tile_of(width, 512)
    for t in range(0, width, tile):
        out_ref[:, t : t + tile] = (factor * dot(codes, turned_ref[:, t : t + tile])).astype(BF16)


def restore_body(codes_ref, turned_ref, out_ref):
    decode(codes_ref[...], turned_ref, out_ref)


def final_body(a_ref, b_ref, turned_ref, out_ref):
    decode((a_ref[...] + b_ref[...]).astype(BF16), turned_ref, out_ref)


def pair_body(x_ref, gate_ref, up_ref, *refs, start):
    keep_ref, send_ref = refs[-2:]
    half = keep_ref.shape[1] // 2
    tile = tile_of(half, 512)
    core = core_index()
    for out_ref, which in ((send_ref, 1 - core), (keep_ref, core)):
        for t in range(0, half, tile):
            at = pl.ds(pl.multiple_of(start + t + which * half, 128), tile)
            out_ref[:, t : t + tile] = dot(x_ref[...], gate_ref[:, at]).astype(out_ref.dtype)
            out_ref[:, half + t : half + t + tile] = dot(x_ref[...], up_ref[:, at]).astype(out_ref.dtype)


def down_body(*refs, parts, first=False):
    h_refs, (weight_ref, *acc, out_ref) = refs[: len(parts)], refs[len(parts) :]
    core = core_index()
    width = out_ref.shape[1]
    tile = tile_of(width, 512)
    for t in range(0, width, tile):
        total = None if first else acc[0][:, t : t + tile]
        for h_ref, (away, start, half) in zip(h_refs, parts):
            at = pl.ds(pl.multiple_of(start + (1 - core if away else core) * half, 16), half)
            part = dot(h_ref[...], weight_ref[at, t : t + tile])
            total = part if total is None else total + part
        out_ref[:, t : t + tile] = total.astype(out_ref.dtype)


def last_body(h_ref, weight_ref, acc_ref, basis_ref, keep_ref, send_ref, rows_ref, *, parts):
    down_body(h_ref, weight_ref, acc_ref, rows_ref, parts=parts)
    top = keep_ref.shape[0]
    tile = tile_of(R, 512)
    for t in range(0, R, tile):
        part = dot(rows_ref[...], basis_ref[:, t : t + tile])
        keep_ref[:, t : t + tile] = part[:top]
        send_ref[:, t : t + tile] = part[top:].astype(BF16)


def both(shape):
    return [sds(shape, F32), sds(shape, BF16)]


def shards(tokens, basis, gate_weight, up_weight, down_weight, *, dp, tensor):
    local, width = tokens.shape
    rows = local * tensor
    ff = gate_weight.shape[1]

    codes, basis = call(
        code_body,
        [sds((local, R), F32), sds(basis.shape, BF16)],
        1,
        tokens,
        basis,
        scratch=[pltpu.VMEM(tokens.shape, BF16), pltpu.SemaphoreType.DMA((PIECES + 1,))],
        fixed=(0, 1),
    )
    codes, send = call(add_two_body, both(codes.shape), WAIT, codes, swap(codes, "dp", 1, dp))
    mask = 2
    while 2 * mask < dp:
        codes, send = call(add_two_body, both(codes.shape), 0.1, codes, swap(send, "dp", mask, dp))
        mask *= 2
    codes = call(add_body, sds(codes.shape, BF16), 0.1, codes, swap(send, "dp", mask, dp))
    mask = 1
    while mask < tensor:
        if 2 * mask == tensor:
            turned = call(turn_body, sds((R, width), BF16), TURN, basis, codes)
        codes = call(
            join_body, sds((2 * codes.shape[0], R), BF16), 0.1, codes, swap(codes, "tensor", mask, tensor)
        )
        mask *= 2
    restored = call(restore_body, sds((rows, width), BF16), 0.5, codes, turned)

    shares = SHARES if ff % 1024 == 0 else (1, 1)
    spans, at = [], 0
    for share in shares:
        spans.append((at, ff * share // sum(shares)))
        at += spans[-1][1]
    pairs, kept, sums = [], [], []
    for q, (start, span) in enumerate(spans):
        keep, send = call(
            functools.partial(pair_body, start=start),
            both((rows, span)),
            PAIRS[q],
            restored,
            gate_weight,
            up_weight,
            *kept[-1:],
            *[send for _, send in sums[-1:]],
        )
        kept.append(keep)
        pairs.append((keep, swap(send, "dp", 1, dp)))
        if q > 0:
            sums.append(call(add_two_body, both((rows, spans[q - 1][1])), SUMS[q - 1], *pairs[q - 1], keep))
    sums.append(call(add_two_body, both((rows, spans[-1][1])), SUMS[-1], *pairs[-1], sums[-1][1]))
    acc, early, own, late = None, None, None, []
    for q, ((start, span), (total, send)) in enumerate(zip(spans, sums)):
        mask = 2
        while 2 * mask < dp:
            total, send = call(add_two_body, both(total.shape), 0.1, total, swap(send, "dp", mask, dp))
            mask *= 2
        half = span // 2
        order = [sums[-1][1]] if q == 0 else [early] if q == 1 else [own]
        own = call(hidden_body, sds((rows, half), BF16), HIDDEN[q], total, swap(send, "dp", mask, dp), *order)
        away = swap(own, "dp", 1, dp)
        blocks = late + [(own, (0, start, half))]
        body = functools.partial(down_body, parts=tuple(part for _, part in blocks), first=acc is None)
        acc = call(
            body, sds((rows, width), F32), DOWN[q], *[h for h, _ in blocks], down_weight, *([] if acc is None else [acc])
        )
        early = acc if early is None else early
        late = [(away, (1, start, half))]
    ((away, part),) = late
    codes, send = call(
        functools.partial(last_body, parts=(part,)),
        [sds((rows // 2, R), F32), sds((rows // 2, R), BF16)],
        1,
        away,
        down_weight,
        acc,
        basis,
        scratch=[pltpu.VMEM((rows, width), BF16)],
    )

    mask = tensor // 2
    while mask > 1:
        top = codes.shape[0] // 2
        codes, send = call(
            half_body, [sds((top, R), F32), sds((top, R), BF16)], 0.1, codes, swap(send, "tensor", mask, tensor)
        )
        mask //= 2
    codes, send = call(add_two_body, both(codes.shape), 0.1, codes, swap(send, "tensor", 1, tensor))
    mask = dp // 2
    while mask > 2:
        codes, send = call(add_two_body, both(codes.shape), 0.1, codes, swap(send, "dp", mask, dp))
        mask //= 2
    codes = call(add_body, sds(codes.shape, F32), 0.1, codes, swap(send, "dp", 2, dp))
    return call(final_body, sds((local, width), BF16), 1, codes, swap(codes, "dp", 1, dp), turned)


SHARES = (2, 1, 1)


def solution(mesh):
    placed = (
        P(("groups", "tensor"), "dp"),
        P("dp", None),
        P("dp", "tensor"),
        P("dp", "tensor"),
        P("tensor", "dp"),
    )
    return jax.shard_map(
        functools.partial(shards, dp=mesh.shape["dp"], tensor=mesh.shape["tensor"]),
        mesh=mesh,
        in_specs=placed,
        out_specs=P(("groups", "tensor"), "dp"),
        check_vma=False,
    )
```
